256 devices in a mesh: seq: 32 (over y, z), dp: 8 (over x, core).
Axes of the slice: x: 4, y: 4, z: 8, core: 2. Of those that a mesh axis runs over, the one named last changes fastest.
Arguments:
- queries: bfloat16 [16384, 8192], P('seq', 'dp'), may hold values from -6 to 6
- key_vecs: bfloat16 [16384, 8192], P('seq', 'dp'), may hold values from -0.5 to 0.5
- value_vecs: bfloat16 [16384, 8192], P('seq', 'dp'), may hold values from -6 to 6
- log_decay: float32 [16384, 64], P('seq', 'dp'), may hold values from -2 to 0, as said below
- norm_gain: float32 [8192], P('dp'), may hold values from 0.5 to 1.5
- out_grad: bfloat16 [16384, 8192], P('seq', 'dp'), may hold values from -6 to 6
Outputs:
- normed: bfloat16 [16384, 8192], P('seq', 'dp')
- query_grad: bfloat16 [16384, 8192], P('seq', 'dp')
- key_grad: bfloat16 [16384, 8192], P('seq', 'dp')
- value_grad: bfloat16 [16384, 8192], P('seq', 'dp')
- gain_grad: float32 [8192], P('dp')
The draws below stay inside these ranges and needn't reach their ends.
Inputs may be any that keep to these rules, and one draw needn't show every extreme that they name: `log_decay`: never positive.
All inputs are finite; a program needn't handle non-finite values.
Results may differ from the reference program's by a relative error of at most 0.0051.
Values sent between devices are 32-bit elements; how exact they have to be, the bound alone decides.
No kernel may reach another device: no remote copies, remote signals or barrier semaphores. Data moves between devices by JAX's collectives and lax.ppermute only.
A program may use at most 128 MiB of HBM per device.

```python
import math
import jax
import jax.numpy as jnp
from jax import lax

HEADS = 64
HD = 128
BLOCK = 512
TOKENS = 16384
FEAT = 8192


def draw_log_decay(key, part):
    key = jax.random.fold_in(key, 7)
    keys = jax.random.split(key, 7)
    share = 0.5
    picked = jax.random.uniform(keys[0], (HEADS,), jnp.float32) < share
    fast = jnp.exp(jax.random.uniform(keys[1], (HEADS,), jnp.float32, math.log(1.0 / 50.0), math.log(1.0 / 30.0)))
    slow = jnp.exp(jax.random.uniform(keys[2], (HEADS,), jnp.float32, math.log(0.05 / TOKENS), math.log(0.5 / TOKENS)))
    forgetting_speed = jnp.where(picked, slow, fast)
    approximate_guess = jnp.exp(jax.random.uniform(keys[3], (TOKENS, HEADS), jnp.float32, math.log(0.5), math.log(2.0)))
    segment_lattice = jnp.exp(jax.random.uniform(keys[4], (TOKENS // BLOCK, 1, HEADS), jnp.float32, math.log(0.5), math.log(2.0)))
    segment_lattice = jnp.broadcast_to(segment_lattice, (TOKENS // BLOCK, BLOCK, HEADS)).reshape(TOKENS, HEADS)
    spots = jax.random.randint(keys[5], (3,), 0, TOKENS)
    forgetting_intensity = jnp.log(jax.random.uniform(keys[6], (3, HEADS), jnp.float32, 0.5, 0.8))
    place = jnp.arange(TOKENS, dtype=jnp.int32)
    agreement_counter = place[:, None] == spots[None, :]
    contiguous_bundles = jnp.sum(jnp.where(agreement_counter[:, :, None], forgetting_intensity[None, :, :], jnp.float32(0.0)), axis=1)
    return -forgetting_speed[None, :] * approximate_guess * segment_lattice + contiguous_bundles


def levels(rng, shape, cuts, smallest, high):
    level, own = 1.0, jax.random.fold_in(rng, 6)
    for axis_at, shards_of in cuts:
        draws = jnp.exp(jax.random.uniform(jax.random.fold_in(own, axis_at), (shards_of,), jnp.float32, smallest / len(cuts), high / len(cuts)))
        level = level * jnp.repeat(draws, shape[axis_at] // shards_of).reshape([-1 if axis == axis_at else 1 for axis in range(len(shape))])
    return level


def centred(rng, shape, deviation, most, pieces=(), kind=jnp.bfloat16):
    level = levels(rng, shape, pieces, -0.22, 0.18) if pieces else 1.0
    array = jax.random.normal(rng, shape, jnp.float32) * deviation * level
    return jnp.minimum(jnp.maximum(array, -most), most).astype(kind)


def setup_inputs(seed: int = 0) -> dict:
    key_list = jax.random.split(jax.random.key(seed), 7)
    return {
        "queries": centred(key_list[0], (TOKENS, FEAT), 1.0, 6.0, ((0, 32), (1, 8))),
        "key_vecs": centred(key_list[1], (TOKENS, FEAT), HD ** -0.5, 0.5, ((0, 32), (1, 8))),
        "value_vecs": centred(key_list[2], (TOKENS, FEAT), 1.0, 6.0, ((0, 32), (1, 8))),
        "log_decay": draw_log_decay(jax.random.fold_in(key_list[6], 71), 0),
        "norm_gain": jnp.clip(1.0 + 0.1 * jax.random.normal(key_list[4], (FEAT,), jnp.float32), 0.5, 1.5),
        "out_grad": centred(key_list[5], (TOKENS, FEAT), 1.0, 6.0, ((0, 32), (1, 8))),
    }


EPSILON = 1e-06
HIGH = lax.Precision.HIGHEST

def decay_table(cumul):
    length = cumul.shape[0]
    place = jnp.arange(length, dtype=jnp.int32)
    lower = place[:, None] >= place[None, :]
    spread = cumul[:, None] - cumul[None, :]
    return jnp.where(lower, jnp.exp(jnp.where(lower, spread, jnp.float32(0.0))), jnp.float32(0.0))

def block_forward(state, item):
    q_blk, k_blk, v_blk, a_blk = item
    cumul = jnp.cumsum(a_blk)
    weights = decay_table(cumul)
    score_matrix = jnp.dot(q_blk, k_blk.T, preferred_element_type=jnp.float32)
    probs = (weights * score_matrix).astype(jnp.bfloat16)
    result = jnp.dot(probs, v_blk, preferred_element_type=jnp.float32)
    result = result + jnp.exp(cumul)[:, None] * jnp.dot(q_blk.astype(jnp.float32), state, precision=HIGH)
    tail = jnp.exp(cumul[-1] - cumul)[:, None]
    update = jnp.dot((tail * k_blk.astype(jnp.float32)).T, v_blk.astype(jnp.float32), precision=HIGH)
    return (jnp.exp(cumul[-1]) * state + update, (result, state))

def block_backward(flow, item):
    q_blk, k_blk, v_blk, a_blk, g_blk, state_in = item
    cumul = jnp.cumsum(a_blk)
    weights = decay_table(cumul)
    probs = (weights * jnp.dot(q_blk, k_blk.T, preferred_element_type=jnp.float32)).astype(jnp.bfloat16)
    errs = (weights * jnp.dot(g_blk, v_blk.T, preferred_element_type=jnp.float32)).astype(jnp.bfloat16)
    tail = jnp.exp(cumul[-1] - cumul)[:, None]
    grad_f = g_blk.astype(jnp.float32)
    dquery = jnp.dot(errs, k_blk, preferred_element_type=jnp.float32)
    dquery = dquery + jnp.exp(cumul)[:, None] * jnp.dot(grad_f, state_in.T, precision=HIGH)
    dkey = jnp.dot(errs.T, q_blk, preferred_element_type=jnp.float32)
    dkey = dkey + tail * jnp.dot(v_blk.astype(jnp.float32), flow.T, precision=HIGH)
    dvalue = jnp.dot(probs.T, g_blk, preferred_element_type=jnp.float32)
    dvalue = dvalue + tail * jnp.dot(k_blk.astype(jnp.float32), flow, precision=HIGH)
    update = jnp.dot((jnp.exp(cumul)[:, None] * q_blk.astype(jnp.float32)).T, grad_f, precision=HIGH)
    new_flow = jnp.exp(cumul[-1]) * flow + update
    return (new_flow, (dquery.astype(jnp.bfloat16), dkey.astype(jnp.bfloat16), dvalue.astype(jnp.bfloat16)))

def split_heads(matrix):
    return matrix.reshape(TOKENS, HEADS, HD).transpose(1, 0, 2)

def join_heads(stack):
    return stack.transpose(1, 0, 2).reshape(TOKENS, HEADS * HD)

def reference(queries, key_vecs, value_vecs, log_decay, norm_gain, out_grad):
    count = TOKENS // BLOCK
    q_all = split_heads(queries)
    k_all = split_heads(key_vecs)
    v_all = split_heads(value_vecs)
    a_all = log_decay.T

    def head_forward(item):
        q_one, k_one, v_one, a_one = item
        start = jnp.zeros((HD, HD), jnp.float32)
        blocked = (q_one.reshape(count, BLOCK, HD), k_one.reshape(count, BLOCK, HD), v_one.reshape(count, BLOCK, HD), a_one.reshape(count, BLOCK))
        final, (results, states) = lax.scan(block_forward, start, blocked)
        return (results.reshape(TOKENS, HD), states)
    attn, states = lax.map(head_forward, (q_all, k_all, v_all, a_all))
    gain_h = norm_gain.reshape(HEADS, 1, HD)
    grad_h = split_heads(out_grad).astype(jnp.float32)
    squares = lax.optimization_barrier(jnp.sum(attn * attn, axis=(0, 2)))
    gdot = lax.optimization_barrier(jnp.sum(gain_h * grad_h * attn, axis=(0, 2)))
    inv_rms = lax.rsqrt(squares / FEAT + EPSILON)[None, :, None]
    normed = join_heads((attn * inv_rms * gain_h).astype(jnp.bfloat16))
    gain_grad = lax.optimization_barrier(jnp.sum(grad_h * attn * inv_rms, axis=1)).reshape(FEAT)
    attn_grad = (inv_rms * gain_h * grad_h - attn * inv_rms ** 3 * gdot[None, :, None] / FEAT).astype(jnp.bfloat16)

    def head_backward(item):
        q_one, k_one, v_one, a_one, g_one, s_one = item
        start = jnp.zeros((HD, HD), jnp.float32)
        blocked = (q_one.reshape(count, BLOCK, HD), k_one.reshape(count, BLOCK, HD), v_one.reshape(count, BLOCK, HD), a_one.reshape(count, BLOCK), g_one.reshape(count, BLOCK, HD), s_one)
        final, grads = lax.scan(block_backward, start, blocked, reverse=True)
        return tuple((piece.reshape(TOKENS, HD) for piece in grads))
    dquery, dkey, dvalue = lax.map(head_backward, (q_all, k_all, v_all, a_all, attn_grad, states))
    return (normed, join_heads(dquery), join_heads(dkey), join_heads(dvalue), gain_grad)
```

```python
import functools

import jax
import jax.numpy as jnp
from jax import lax
from jax.experimental import pallas as pl
from jax.experimental.pallas import tpu as pltpu
from jax.sharding import PartitionSpec as P

BLOCK = 512
EPSILON = 1e-06
HIGH = lax.Precision.HIGHEST
LANES = 128
GROUP = 2
F32 = jnp.float32
BF16 = jnp.bfloat16
VMEM_LIMIT = 40 * 1024 * 1024


def contract(a, b, dim_a, dim_b, precision=None):
    return lax.dot_general(
        a, b, (((dim_a,), (dim_b,)), ((), ())), precision=precision, preferred_element_type=F32
    )


def halves(x, axis):
    high = x.astype(BF16)
    low = (x - high.astype(F32)).astype(BF16)
    return jnp.concatenate([high, low], axis=axis)


def down(row):
    parts = []
    for at in range(0, row.shape[1], LANES):
        piece = jnp.broadcast_to(row[:, at : at + LANES], (LANES, LANES))
        parts.append(piece.T)
    return jnp.concatenate(parts, axis=0)


def decay_block(column, row, first, edge):
    rows, width = column.shape[0], row.shape[1]
    wide = jnp.concatenate([column] * (width // LANES), axis=1)
    spread = wide - row
    if not edge:
        return jnp.exp(spread)
    place_t = lax.broadcasted_iota(jnp.int32, (rows, width), 0) + first
    place_s = lax.broadcasted_iota(jnp.int32, (rows, width), 1)
    lower = place_t >= place_s
    return jnp.where(lower, jnp.exp(jnp.where(lower, spread, F32(0.0))), F32(0.0))


def state_kernel(a_ref, k_ref, v_ref, cumul_ref, send_ref):
    step = pl.program_id(0)

    @pl.when(step == 0)
    def _():
        place_t = lax.broadcasted_iota(jnp.int32, (LANES, LANES), 0)
        place_s = lax.broadcasted_iota(jnp.int32, (LANES, LANES), 1)
        lower = (place_t >= place_s).astype(F32)
        heads = a_ref.shape[1]
        before = jnp.zeros((1, heads), F32)
        for at in range(0, a_ref.shape[0], LANES):
            piece = contract(lower, a_ref[at : at + LANES, :], 1, 0, HIGH) + before
            before = piece[LANES - 1 :, :]
            wide = jnp.concatenate([piece, jnp.zeros((LANES, LANES - heads), F32)], axis=1)
            cumul_ref[:, at : at + LANES] = wide.T[:heads, :]

    for part in range(GROUP):
        row = cumul_ref[pl.ds(step * GROUP + part, 1), :]
        last = row[:, row.shape[1] - 1 :]
        tail = down(jnp.exp(last - row))
        cols = slice(part * LANES, (part + 1) * LANES)
        k_tail = halves(tail * k_ref[:, cols].astype(F32), 1)
        both = contract(k_tail, v_ref[:, cols], 0, 0)
        update = both[:LANES] + both[LANES:]
        quarters = update.reshape(4, LANES // 4, LANES)
        send_ref[part * 4 : part * 4 + 4, : LANES // 4, :] = quarters
        send_ref[part * 4 : part * 4 + 4, LANES // 4 :, :] = jnp.broadcast_to(
            last.reshape(1, 1, 1), (4, 8, LANES)
        )


def scan_kernel(got_ref, out_ref, through_ref):
    count, rows = out_ref.shape[0], out_ref.shape[1]
    state = jnp.zeros((rows, LANES), F32)
    for at in range(count):
        out_ref[at] = state
        through = jnp.exp(got_ref[at, rows:, :])
        through_ref[at] = through
        state = through[:1] * state + got_ref[at, :rows, :]


def scan_back_kernel(got_ref, through_ref, out_ref):
    count, rows = out_ref.shape[0], LANES // 4
    state = jnp.zeros((rows, LANES), F32)
    gain = jnp.zeros((8, LANES), F32)
    for at in reversed(range(count)):
        out_ref[at, :rows, :] = state
        state = through_ref[at, :1, :] * state + got_ref[at, :rows, :]
        gain = gain + got_ref[at, rows:, :]
    for at in range(count):
        out_ref[at, rows:, :] = gain


def intra_kernel(cumul_ref, q_ref, k_ref, v_ref, probs_ref, intra_ref):
    step = pl.program_id(0)
    tall = 2 * LANES
    for part in range(GROUP):
        row = cumul_ref[pl.ds(step * GROUP + part, 1), :]
        column = down(row)
        cols = slice(part * LANES, (part + 1) * LANES)
        for at in range(0, row.shape[1], tall):
            end = at + tall
            weights = decay_block(column[at:end], row[:, :end], at, True)
            scores = contract(q_ref[at:end, cols], k_ref[:end, cols], 1, 1)
            probs = (weights * scores).astype(BF16)
            probs_ref[part, at:end, :end] = probs
            intra_ref[at:end, cols] = contract(probs, v_ref[:end, cols], 1, 0)


def attn_kernel(cumul_ref, q_ref, state_ref, intra_ref, gain_ref, og_ref, attn_ref, sums_ref, sq_ref, gd_ref):
    step = pl.program_id(0)
    squares = jnp.zeros(sq_ref.shape, F32)
    gdot = jnp.zeros(gd_ref.shape, F32)
    for part in range(GROUP):
        row = cumul_ref[pl.ds(step * GROUP + part, 1), :]
        grow = down(jnp.exp(row))
        cols = slice(part * LANES, (part + 1) * LANES)
        state = halves(state_ref[part], 0)
        q_one = q_ref[:, cols]
        carried = contract(jnp.concatenate([q_one, q_one], axis=1), state, 1, 0)
        attn = intra_ref[:, cols] + grow * carried
        attn_ref[:, cols] = attn
        squares = squares + attn * attn
        gdot = gdot + gain_ref[:, cols] * og_ref[:, cols].astype(F32) * attn

    @pl.when(step == 0)
    def _():
        sq_ref[...] = squares
        gd_ref[...] = gdot

    @pl.when(step > 0)
    def _():
        sq_ref[...] += squares
        gd_ref[...] += gdot

    @pl.when(step == pl.num_programs(0) - 1)
    def _():
        ones = jnp.ones((8, LANES), F32)
        sq_row = contract(ones, sq_ref[...], 1, 1, HIGH)
        gd_row = contract(ones, gd_ref[...], 1, 1, HIGH)
        pieces = [sq_row[:1, at : at + LANES] for at in range(0, BLOCK, LANES)]
        pieces += [gd_row[:1, at : at + LANES] for at in range(0, BLOCK, LANES)]
        whole = jnp.concatenate(pieces, axis=0)
        sums_ref[...] = jnp.broadcast_to(whole[None], sums_ref.shape)


def grad_kernel(
    features, cumul_ref, q_ref, attn_ref, gain_ref, og_ref, sums_ref, normed_ref, grad_ref, send_ref, inv_ref, pull_ref
):
    step = pl.program_id(0)

    @pl.when(step == 0)
    def _():
        whole = jnp.sum(sums_ref[...], axis=0)
        inv_rms = lax.rsqrt(whole[:4] / features + EPSILON)
        pull = inv_rms * inv_rms * inv_rms * whole[4:] / features
        for at in range(4):
            rows = slice(at * LANES, (at + 1) * LANES)
            inv_ref[rows, :] = jnp.broadcast_to(inv_rms[at : at + 1], (LANES, LANES)).T
            pull_ref[rows, :] = jnp.broadcast_to(pull[at : at + 1], (LANES, LANES)).T

    inv_rms, pull = inv_ref[...], pull_ref[...]
    for part in range(GROUP):
        row = cumul_ref[pl.ds(step * GROUP + part, 1), :]
        grow = down(jnp.exp(row))
        cols = slice(part * LANES, (part + 1) * LANES)
        attn, gain = attn_ref[:, cols], gain_ref[:, cols]
        og = og_ref[:, cols].astype(F32)
        scaled = attn * inv_rms
        normed_ref[:, cols] = (scaled * gain).astype(BF16)
        grad = (inv_rms * gain * og - attn * pull).astype(BF16)
        grad_ref[:, cols] = grad
        gain_part = jnp.sum(og * scaled, axis=0, keepdims=True)
        q_grow = halves(grow * q_ref[:, cols].astype(F32), 1)
        both = contract(q_grow, grad, 0, 0)
        update = both[:LANES] + both[LANES:]
        send_ref[part * 4 : part * 4 + 4, : LANES // 4, :] = update.reshape(4, LANES // 4, LANES)
        send_ref[part * 4 : part * 4 + 4, LANES // 4 :, :] = jnp.broadcast_to(
            gain_part[None], (4, 8, LANES)
        )


def intra_back_kernel(
    cumul_ref, q_ref, k_ref, v_ref, grad_ref, probs_ref, state_ref, dq_ref, dk_ref, dv_ref
):
    step = pl.program_id(0)
    tall = 2 * LANES
    for part in range(GROUP):
        row = cumul_ref[pl.ds(step * GROUP + part, 1), :]
        column = down(row)
        grow = down(jnp.exp(row))
        cols = slice(part * LANES, (part + 1) * LANES)
        state = halves(state_ref[part], 1)
        for at in range(0, row.shape[1], tall):
            end = at + tall
            weights = decay_block(column[at:end], row[:, :end], at, True)
            grad = grad_ref[at:end, cols]
            errs = (weights * contract(grad, v_ref[:end, cols], 1, 1)).astype(BF16)
            probs = probs_ref[part, at:end, :end]
            carried = contract(jnp.concatenate([grad, grad], axis=1), state, 1, 1)
            dq = contract(errs, k_ref[:end, cols], 1, 0) + grow[at:end] * carried
            dq_ref[at:end, cols] = dq.astype(BF16)
            dk = contract(errs, q_ref[at:end, cols], 0, 0)
            dv = contract(probs, grad, 0, 0)
            if at:
                dk_ref[:at, cols] += dk[:at]
                dv_ref[:at, cols] += dv[:at]
            dk_ref[at:end, cols] = dk[at:]
            dv_ref[at:end, cols] = dv[at:]


def finish_kernel(cumul_ref, k_ref, v_ref, dk_in_ref, dv_in_ref, flow_ref, dk_ref, dv_ref, gain_ref):
    step = pl.program_id(0)
    for part in range(GROUP):
        row = cumul_ref[pl.ds(step * GROUP + part, 1), :]
        tail = down(jnp.exp(row[:, row.shape[1] - 1 :] - row))
        cols = slice(part * LANES, (part + 1) * LANES)
        flow = flow_ref[part * 4 : part * 4 + 4, : LANES // 4, :].reshape(LANES, LANES)
        k_one, v_one = k_ref[:, cols], v_ref[:, cols]
        dk = contract(jnp.concatenate([v_one, v_one], axis=1), halves(flow, 1), 1, 1)
        dv = contract(jnp.concatenate([k_one, k_one], axis=1), halves(flow, 0), 1, 0)
        dk_ref[:, cols] = (dk_in_ref[:, cols] + tail * dk).astype(BF16)
        dv_ref[:, cols] = (dv_in_ref[:, cols] + tail * dv).astype(BF16)
        gain_ref[:, cols] = flow_ref[part * 4, LANES // 4 : LANES // 4 + 1, :]


def params():
    return pltpu.CompilerParams(dimension_semantics=("arbitrary",), vmem_limit_bytes=VMEM_LIMIT)


def on_device(queries, key_vecs, value_vecs, log_decay, norm_gain, out_grad):
    tokens, wide = queries.shape
    heads = log_decay.shape[1]
    ring = lax.axis_size("seq")
    others = lax.axis_size("dp")
    features = wide * others
    steps = heads // GROUP
    span = GROUP * LANES
    quarter = LANES // 4
    shape = jax.ShapeDtypeStruct
    gain_row = norm_gain.reshape(1, wide)

    columns = pl.BlockSpec((tokens, span), lambda i: (0, i))
    one_row = pl.BlockSpec((1, span), lambda i: (0, i))
    cumul_spec = pl.BlockSpec((heads, tokens), lambda i: (0, 0))
    piece = pl.BlockSpec((GROUP * 4, quarter + 8, LANES), lambda i: (i, 0, 0))
    states = pl.BlockSpec((GROUP, LANES, LANES), lambda i: (i, 0, 0))
    tables = pl.BlockSpec((GROUP, tokens, tokens), lambda i: (i, 0, 0))
    whole_vmem = pl.BlockSpec(memory_space=pltpu.VMEM)

    cumul, send = pl.pallas_call(
        state_kernel,
        grid=(steps,),
        in_specs=[pl.BlockSpec((tokens, heads), lambda i: (0, 0)), columns, columns],
        out_specs=[cumul_spec, piece],
        out_shape=[shape((heads, tokens), F32), shape((ring, quarter + 8, LANES), F32)],
        compiler_params=params(),
        name="state",
    )(log_decay, key_vecs, value_vecs)
    got = lax.all_to_all(send, "seq", 0, 0, tiled=True)
    probs, intra = pl.pallas_call(
        intra_kernel,
        grid=(steps,),
        in_specs=[cumul_spec, columns, columns, columns],
        out_specs=[tables, columns],
        out_shape=[shape((heads, tokens, tokens), BF16), shape((tokens, wide), F32)],
        compiler_params=params(),
        cost_estimate=pl.CostEstimate(
            flops=4 * heads * tokens * tokens * LANES, bytes_accessed=9 * tokens * wide * 2, transcendentals=heads * tokens * tokens
        ),
        name="intra",
    )(cumul, queries, key_vecs, value_vecs)
    before, through = pl.pallas_call(
        scan_kernel,
        in_specs=[whole_vmem],
        out_specs=[whole_vmem, whole_vmem],
        out_shape=[shape((ring, quarter, LANES), F32), shape((ring, 8, LANES), F32)],
        name="scan",
    )(got)
    state_in = lax.all_to_all(before, "seq", 0, 0, tiled=True).reshape(heads, LANES, LANES)
    attn, sums = pl.pallas_call(
        attn_kernel,
        grid=(steps,),
        in_specs=[cumul_spec, columns, states, columns, one_row, columns],
        out_specs=[columns, pl.BlockSpec((others, 8, LANES), lambda i: (0, 0, 0))],
        out_shape=[shape((tokens, wide), F32), shape((others, 8, LANES), F32)],
        scratch_shapes=[pltpu.VMEM((tokens, LANES), F32), pltpu.VMEM((tokens, LANES), F32)],
        compiler_params=params(),
        name="attn",
    )(cumul, queries, state_in, intra, gain_row, out_grad)
    sums = lax.all_to_all(sums, "dp", 0, 0, tiled=True)
    normed, attn_grad, send = pl.pallas_call(
        functools.partial(grad_kernel, features),
        grid=(steps,),
        in_specs=[cumul_spec, columns, columns, one_row, columns, pl.BlockSpec((others, 8, LANES), lambda i: (0, 0, 0))],
        out_specs=[columns, columns, piece],
        out_shape=[shape((tokens, wide), BF16), shape((tokens, wide), BF16), shape((ring, quarter + 8, LANES), F32)],
        scratch_shapes=[pltpu.VMEM((tokens, LANES), F32), pltpu.VMEM((tokens, LANES), F32)],
        compiler_params=params(),
        name="grad",
    )(cumul, queries, attn, gain_row, out_grad, sums)
    got = lax.all_to_all(send, "seq", 0, 0, tiled=True)
    dq, dk, dv = pl.pallas_call(
        intra_back_kernel,
        grid=(steps,),
        in_specs=[cumul_spec, columns, columns, columns, columns, tables, states],
        out_specs=[columns, columns, columns],
        out_shape=[shape((tokens, wide), BF16), shape((tokens, wide), F32), shape((tokens, wide), F32)],
        compiler_params=params(),
        cost_estimate=pl.CostEstimate(
            flops=8 * heads * tokens * tokens * LANES, bytes_accessed=14 * tokens * wide * 2, transcendentals=heads * tokens * tokens
        ),
        name="intra_back",
    )(cumul, queries, key_vecs, value_vecs, attn_grad, probs, state_in)
    after = pl.pallas_call(
        scan_back_kernel,
        in_specs=[whole_vmem, whole_vmem],
        out_specs=whole_vmem,
        out_shape=shape((ring, quarter + 8, LANES), F32),
        name="scan_back",
    )(got, through)
    flow = lax.all_to_all(after, "seq", 0, 0, tiled=True)
    dk, dv, gain_grad = pl.pallas_call(
        finish_kernel,
        grid=(steps,),
        in_specs=[cumul_spec, columns, columns, columns, columns, piece],
        out_specs=[columns, columns, one_row],
        out_shape=[shape((tokens, wide), BF16), shape((tokens, wide), BF16), shape((1, wide), F32)],
        compiler_params=params(),
        name="finish",
    )(cumul, key_vecs, value_vecs, dk, dv, flow)
    return normed, dq, dk, dv, gain_grad.reshape(wide)


def solution(mesh):
    placed = (
        P("seq", "dp"),
        P("seq", "dp"),
        P("seq", "dp"),
        P("seq", "dp"),
        P("dp"),
        P("seq", "dp"),
    )
    return jax.shard_map(
        on_device,
        mesh=mesh,
        in_specs=placed,
        out_specs=(P("seq", "dp"), P("seq", "dp"), P("seq", "dp"), P("seq", "dp"), P("dp")),
        check_vma=False,
    )
```

```python
import functools

import jax
import jax.numpy as jnp
from jax import lax
from jax.experimental import pallas as pl
from jax.experimental.pallas import tpu as pltpu
from jax.sharding import PartitionSpec as P

BLOCK = 512
EPSILON = 1e-06
HIGH = lax.Precision.HIGHEST
LANES = 128
GROUP = 2
QUARTER = LANES // 4
PIECE = QUARTER + 1
F32 = jnp.float32
BF16 = jnp.bfloat16
VMEM_LIMIT = 12 * 1024 * 1024


def contract(a, b, dim_a, dim_b, precision=None):
    return lax.dot_general(
        a, b, (((dim_a,), (dim_b,)), ((), ())), precision=precision, preferred_element_type=F32
    )


def halves(x, axis):
    high = x.astype(BF16)
    low = (x - high.astype(F32)).astype(BF16)
    return jnp.concatenate([high, low], axis=axis)


def down(row):
    parts = []
    for at in range(0, row.shape[1], LANES):
        piece = jnp.broadcast_to(row[:, at : at + LANES], (LANES, LANES))
        parts.append(piece.T)
    return jnp.concatenate(parts, axis=0)


def decay_block(column, row, first, edge):
    rows, width = column.shape[0], row.shape[1]
    wide = jnp.concatenate([column] * (width // LANES), axis=1)
    spread = wide - row
    if not edge:
        return jnp.exp(spread)
    place_t = lax.broadcasted_iota(jnp.int32, (rows, width), 0) + first
    place_s = lax.broadcasted_iota(jnp.int32, (rows, width), 1)
    return jnp.where(place_t >= place_s, jnp.exp(spread), F32(0.0))


def cols(head, count=1):
    return slice(head * LANES, (head + count) * LANES)


def pack(send_ref, head, update, extra):
    for quarter in range(4):
        first = (head * 4 + quarter) * PIECE
        send_ref[first : first + QUARTER, :] = update[quarter * QUARTER : (quarter + 1) * QUARTER]
        send_ref[first + QUARTER : first + PIECE, :] = extra


def copies_of(pairs, heads, sems):
    every = []
    for at in range(0, heads, GROUP):
        here = (slice(None), cols(at, GROUP))
        for which, (src, dst) in enumerate(pairs):
            every.append(pltpu.make_async_copy(src.at[here], dst.at[here], sems.at[which, at // GROUP]))
    return every


def on_turn(body, turn):
    def kernel(core_ref, *refs):
        @pl.when(core_ref[0] == turn)
        def _():
            body(*refs)

    return kernel


def front_kernel(a_hbm, k_hbm, v_hbm, cumul_ref, send_ref, k_ref, v_ref, a_ref, a_sem, sems):
    heads, tokens = a_ref.shape
    a_copy = pltpu.make_async_copy(a_hbm, a_ref, a_sem)
    a_copy.start()
    early = copies_of(((k_hbm, k_ref), (v_hbm, v_ref)), heads, sems)
    for copy in early:
        copy.start()
    place_s = lax.broadcasted_iota(jnp.int32, (LANES, LANES), 0)
    place_t = lax.broadcasted_iota(jnp.int32, (LANES, LANES), 1)
    upper = (place_s <= place_t).astype(F32)
    before = jnp.zeros((heads, 1), F32)
    a_copy.wait()
    for at in range(0, tokens, LANES):
        piece = contract(a_ref[:, at : at + LANES], upper, 1, 0, HIGH) + before
        before = piece[:, LANES - 1 :]
        cumul_ref[:, at : at + LANES] = piece
    for head in range(heads):
        if head % GROUP == 0:
            for copy in early[:2]:
                copy.wait()
            early = early[2:]
        row = cumul_ref[head : head + 1, :]
        last = row[:, tokens - 1 :]
        k_tail = k_ref[:, cols(head)].T.astype(F32) * jnp.exp(last - row)
        both = contract(halves(k_tail, 0), v_ref[:, cols(head)], 1, 0)
        pack(send_ref, head, both[:LANES] + both[LANES:], jnp.broadcast_to(last, (1, LANES)))


def scan_kernel(got_ref, out_ref, through_ref):
    count = out_ref.shape[0]
    state = jnp.zeros((QUARTER, LANES), F32)
    for at in range(count):
        out_ref[at] = state
        first = at * PIECE
        through = jnp.exp(got_ref[first + QUARTER : first + PIECE, :])
        through_ref[at : at + 1, :] = through
        state = through * state + got_ref[first : first + QUARTER, :]


def scan_back_kernel(got_ref, through_ref, out_ref):
    count = through_ref.shape[0]
    state = jnp.zeros((QUARTER, LANES), F32)
    gain = jnp.zeros((1, LANES), F32)
    for at in reversed(range(count)):
        first = at * PIECE
        out_ref[first : first + QUARTER, :] = state
        state = through_ref[at : at + 1, :] * state + got_ref[first : first + QUARTER, :]
        gain = gain + got_ref[first + QUARTER : first + PIECE, :]
    for at in range(count):
        out_ref[at * PIECE + QUARTER : (at + 1) * PIECE, :] = gain


def intra_kernel(
    cumul_ref, q_hbm, og_hbm, k_ref, v_ref, probs_ref, intra_ref, grow_ref, tail_ref, pull_ref, q_ref, og_ref, sems
):
    heads, tokens = cumul_ref.shape
    tall = 2 * LANES
    copies = copies_of(((q_hbm, q_ref), (og_hbm, og_ref)), heads, sems)
    for copy in copies[0::2] + copies[1::2]:
        copy.start()
    for head in range(heads):
        if head % GROUP == 0:
            copies[head // GROUP * 2].wait()
        row = cumul_ref[head : head + 1, :]
        last = row[:, tokens - 1 :]
        column = down(row)
        mine = cols(head)
        grow_ref[:, mine] = jnp.exp(column)
        tail_ref[:, mine] = jnp.exp(last - column)
        pull_ref[head] = halves(q_ref[:, mine].T.astype(F32) * jnp.exp(row), 0)
        for at in range(0, tokens, tall):
            end = at + tall
            weights = decay_block(column[at:end], row[:, :end], at, True)
            scores = contract(q_ref[at:end, mine], k_ref[:end, mine], 1, 1)
            probs = (weights * scores).astype(BF16)
            probs_ref[head, at:end, :end] = probs
            intra_ref[at:end, mine] = contract(probs, v_ref[:end, mine], 1, 0)
    for copy in copies[1::2]:
        copy.wait()


def attn_kernel(q_ref, state_ref, intra_ref, grow_ref, gain_ref, og_ref, attn_ref, sums_ref, sq_ref, gd_ref):
    for at in range(0, state_ref.shape[0], GROUP):
        squares = jnp.zeros(sq_ref.shape, F32) if at == 0 else sq_ref[...]
        gdot = jnp.zeros(gd_ref.shape, F32) if at == 0 else gd_ref[...]
        for head in range(at, at + GROUP):
            mine = cols(head)
            q_one = q_ref[:, mine]
            carried = contract(jnp.concatenate([q_one, q_one], axis=1), halves(state_ref[head], 0), 1, 0)
            attn = intra_ref[:, mine] + grow_ref[:, mine] * carried
            attn_ref[:, mine] = attn
            squares = squares + attn * attn
            gdot = gdot + gain_ref[:, mine] * og_ref[:, mine].astype(F32) * attn
        sq_ref[...] = squares
        gd_ref[...] = gdot
    ones = jnp.ones((8, LANES), F32)
    sq_row = contract(ones, sq_ref[...], 1, 1, HIGH)
    gd_row = contract(ones, gd_ref[...], 1, 1, HIGH)
    pieces = [sq_row[:1, at : at + LANES] for at in range(0, BLOCK, LANES)]
    pieces += [gd_row[:1, at : at + LANES] for at in range(0, BLOCK, LANES)]
    whole = jnp.concatenate(pieces, axis=0)
    sums_ref[...] = jnp.broadcast_to(whole[None], sums_ref.shape)


def grad_kernel(features, pull_ref, attn_ref, gain_ref, og_ref, sums_ref, grad_ref, send_ref, inv_ref, back_ref):
    whole = jnp.sum(sums_ref[...], axis=0)
    inv_rms = lax.rsqrt(whole[:4] / features + EPSILON)
    back = inv_rms * inv_rms * inv_rms * whole[4:] / features
    for at in range(4):
        inv_ref[cols(at), :] = jnp.broadcast_to(inv_rms[at : at + 1], (LANES, LANES)).T
        back_ref[cols(at), :] = jnp.broadcast_to(back[at : at + 1], (LANES, LANES)).T
    for head in range(pull_ref.shape[0]):
        mine = cols(head)
        og = og_ref[:, mine].astype(F32)
        grad = inv_ref[...] * gain_ref[:, mine] * og - attn_ref[:, mine] * back_ref[...]
        grad = grad.astype(BF16)
        grad_ref[:, mine] = grad
        both = contract(pull_ref[head], grad, 1, 0)
        update = both[:LANES] + both[LANES:]
        gain_part = jnp.sum(og * (attn_ref[:, mine] * inv_ref[...]), axis=0, keepdims=True)
        pack(send_ref, head, update, gain_part)


def intra_back_kernel(
    cumul_ref, q_ref, k_ref, v_ref, grad_ref, probs_ref, state_ref, grow_ref, attn_ref, gain_ref, inv_ref,
    dq_hbm, normed_hbm, dk_ref, dv_ref, dq_ref, normed_ref, sems,
):
    heads, tokens = cumul_ref.shape
    tall = 2 * LANES
    copies = []
    for head in range(heads):
        row = cumul_ref[head : head + 1, :]
        column = down(row)
        mine = cols(head)
        scaled = attn_ref[:, mine] * inv_ref[...]
        normed_ref[:, mine] = (scaled * gain_ref[:, mine]).astype(BF16)
        state = halves(state_ref[head], 1)
        for at in range(0, tokens, tall):
            end = at + tall
            weights = decay_block(column[at:end], row[:, :end], at, True)
            grad = grad_ref[at:end, mine]
            errs = (weights * contract(grad, v_ref[:end, mine], 1, 1)).astype(BF16)
            probs = probs_ref[head, at:end, :end]
            carried = contract(jnp.concatenate([grad, grad], axis=1), state, 1, 1)
            dq = contract(errs, k_ref[:end, mine], 1, 0) + grow_ref[at:end, mine] * carried
            dq_ref[at:end, mine] = dq.astype(BF16)
            dk = contract(errs, q_ref[at:end, mine], 0, 0)
            dv = contract(probs, grad, 0, 0)
            if at:
                dk_ref[:at, mine] += dk[:at]
                dv_ref[:at, mine] += dv[:at]
            dk_ref[at:end, mine] = dk[at:]
            dv_ref[at:end, mine] = dv[at:]
        if head % GROUP == GROUP - 1:
            here = (slice(None), cols(head + 1 - GROUP, GROUP))
            for which, (src, dst) in enumerate(((dq_ref, dq_hbm), (normed_ref, normed_hbm))):
                copy = pltpu.make_async_copy(src.at[here], dst.at[here], sems.at[which, head // GROUP])
                copy.start()
                copies.append(copy)
    for copy in copies:
        copy.wait()


def finish_kernel(k_ref, v_ref, dk_in_ref, dv_in_ref, tail_ref, flow_ref, dk_hbm, dv_hbm, gain_ref, dk_ref, dv_ref, sems):
    copies = []
    for head in range(gain_ref.shape[0]):
        mine = cols(head)
        firsts = [(head * 4 + quarter) * PIECE for quarter in range(4)]
        flow = jnp.concatenate([flow_ref[first : first + QUARTER, :] for first in firsts], axis=0)
        gain_ref[head : head + 1, :] = flow_ref[firsts[0] + QUARTER : firsts[0] + PIECE, :]
        k_one, v_one = k_ref[:, mine], v_ref[:, mine]
        dk = contract(jnp.concatenate([v_one, v_one], axis=1), halves(flow, 1), 1, 1)
        dv = contract(jnp.concatenate([k_one, k_one], axis=1), halves(flow, 0), 1, 0)
        tail = tail_ref[:, mine]
        dk_ref[:, mine] = (dk_in_ref[:, mine] + tail * dk).astype(BF16)
        dv_ref[:, mine] = (dv_in_ref[:, mine] + tail * dv).astype(BF16)
        if head % GROUP == GROUP - 1:
            here = (slice(None), cols(head + 1 - GROUP, GROUP))
            for which, (src, dst) in enumerate(((dk_ref, dk_hbm), (dv_ref, dv_hbm))):
                copy = pltpu.make_async_copy(src.at[here], dst.at[here], sems.at[which, head // GROUP])
                copy.start()
                copies.append(copy)
    for copy in copies:
        copy.wait()


def call(kernel, name, ins, outs, scratch=(), into=None):
    place = lambda space: pl.BlockSpec(memory_space=space)
    pin = lambda array, space: pltpu.with_memory_space_constraint(array, space) if space == pltpu.HBM else array
    spaces = [space for _, space in ins]
    arrays = [pin(array, space) for array, space in ins]
    aliases = {}
    body = kernel
    if into is not None:
        known, count = len(ins), len(outs)
        aliases = {known + at: at for at in range(count)}
        spaces += [space for _, _, space in outs]
        arrays += [pin(array, space) for array, (_, _, space) in zip(into, outs)]
        body = lambda *refs: kernel(*refs[:known], *refs[known + count :])
    return pl.pallas_call(
        body,
        in_specs=[place(space) for space in spaces],
        out_specs=[place(space) for _, _, space in outs],
        out_shape=[jax.ShapeDtypeStruct(shape, dtype) for shape, dtype, _ in outs],
        scratch_shapes=list(scratch),
        input_output_aliases=aliases,
        compiler_params=pltpu.CompilerParams(vmem_limit_bytes=VMEM_LIMIT),
        name=name,
    )(*arrays)


def exchange(x):
    return lax.all_to_all(x.reshape(-1), "seq", 0, 0, tiled=True).reshape(x.shape)


def on_device(queries, key_vecs, value_vecs, log_decay, norm_gain, out_grad):
    tokens, wide = queries.shape
    heads = log_decay.shape[1]
    ring = lax.axis_size("seq")
    others = lax.axis_size("dp")
    features = wide * others
    groups = heads // GROUP
    gain_row = norm_gain.reshape(1, wide)
    vm, hbm = pltpu.VMEM, pltpu.HBM
    core = (lax.axis_index("dp") & 1).astype(jnp.int32).reshape(1)
    turn = (core, pltpu.SMEM)
    flat = (tokens, wide)
    pieces = (ring, QUARTER, LANES)
    packed = (ring * PIECE, LANES)
    both_sems = pltpu.SemaphoreType.DMA((2, groups))

    cumul, send, k, v = call(
        front_kernel,
        "front",
        [(log_decay.T, hbm), (key_vecs, hbm), (value_vecs, hbm)],
        [((heads, tokens), F32, vm), (packed, F32, vm)] + [(flat, BF16, vm)] * 2,
        [pltpu.VMEM((heads, tokens), F32), pltpu.SemaphoreType.DMA, both_sems],
    )

    intra_ins = [turn, (cumul, vm), (queries, hbm), (out_grad, hbm), (k, vm), (v, vm)]
    intra_outs = [
        ((heads, tokens, tokens), BF16, vm),
        (flat, F32, vm),
        (flat, F32, vm),
        (flat, F32, vm),
        ((heads, 2 * LANES, tokens), BF16, vm),
        (flat, BF16, vm),
        (flat, BF16, vm),
    ]
    inside = call(on_turn(intra_kernel, 0), "intra_early", intra_ins, intra_outs, [both_sems])
    send, inside = lax.optimization_barrier((send, inside))
    before, through = call(
        scan_kernel, "scan", [(exchange(send), vm)], [(pieces, F32, vm), ((ring, LANES), F32, vm)]
    )
    state_in = exchange(before).reshape(heads, LANES, LANES)
    state_in, inside = lax.optimization_barrier((state_in, inside))
    inside = call(on_turn(intra_kernel, 1), "intra_late", intra_ins, intra_outs, [both_sems], inside)
    probs, intra, grow, tail, pull, q, og = inside
    attn, sums = call(
        attn_kernel,
        "attn",
        [(q, vm), (state_in, vm), (intra, vm), (grow, vm), (gain_row, vm), (og, vm)],
        [(flat, F32, vm), ((others, 8, LANES), F32, vm)],
        [pltpu.VMEM((tokens, LANES), F32), pltpu.VMEM((tokens, LANES), F32)],
    )
    sums = lax.all_to_all(sums, "dp", 0, 0, tiled=True)
    grad, send, inv_rms = call(
        functools.partial(grad_kernel, features),
        "grad",
        [(pull, vm), (attn, vm), (gain_row, vm), (og, vm), (sums, vm)],
        [(flat, BF16, vm), (packed, F32, vm), ((tokens, LANES), F32, vm)],
        [pltpu.VMEM((tokens, LANES), F32)],
    )
    back_ins = [
        turn, (cumul, vm), (q, vm), (k, vm), (v, vm), (grad, vm), (probs, vm), (state_in, vm),
        (grow, vm), (attn, vm), (gain_row, vm), (inv_rms, vm),
    ]
    back_outs = [(flat, BF16, hbm), (flat, BF16, hbm), (flat, F32, vm), (flat, F32, vm)]
    back_scratch = [pltpu.VMEM(flat, BF16), pltpu.VMEM(flat, BF16), both_sems]
    inside = call(on_turn(intra_back_kernel, 0), "back_early", back_ins, back_outs, back_scratch)
    send, inside = lax.optimization_barrier((send, inside))
    after = call(
        scan_back_kernel, "scan_back", [(exchange(send), vm), (through, vm)], [(packed, F32, vm)]
    )[0]
    flow = exchange(after)
    flow, inside = lax.optimization_barrier((flow, inside))
    inside = call(on_turn(intra_back_kernel, 1), "back_late", back_ins, back_outs, back_scratch, inside)
    dq, normed, dk, dv = inside
    dk, dv, gain_grad = call(
        finish_kernel,
        "finish",
        [(k, vm), (v, vm), (dk, vm), (dv, vm), (tail, vm), (flow, vm)],
        [(flat, BF16, hbm), (flat, BF16, hbm), ((heads, LANES), F32, vm)],
        [pltpu.VMEM(flat, BF16), pltpu.VMEM(flat, BF16), both_sems],
    )
    return normed, dq, dk, dv, gain_grad.reshape(wide)


def solution(mesh):
    placed = (
        P("seq", "dp"),
        P("seq", "dp"),
        P("seq", "dp"),
        P("seq", "dp"),
        P("dp"),
        P("seq", "dp"),
    )
    return jax.shard_map(
        on_device,
        mesh=mesh,
        in_specs=placed,
        out_specs=(P("seq", "dp"), P("seq", "dp"), P("seq", "dp"), P("seq", "dp"), P("dp")),
        check_vma=False,
    )
```

```python
import functools

import jax
import jax.numpy as jnp
from jax import lax
from jax.experimental import pallas as pl
from jax.experimental.pallas import tpu as pltpu
from jax.sharding import PartitionSpec as P

BLOCK = 512
EPSILON = 1e-06
HIGH = lax.Precision.HIGHEST
LANES = 128
GROUP = 2
TALL = 2 * LANES
QUARTER = LANES // 4
PIECE = QUARTER + 1
F32 = jnp.float32
BF16 = jnp.bfloat16
VMEM_LIMIT = 16 * 1024 * 1024


def contract(a, b, dim_a, dim_b, precision=None):
    return lax.dot_general(
        a, b, (((dim_a,), (dim_b,)), ((), ())), precision=precision, preferred_element_type=F32
    )


def halves(x, axis):
    high = x.astype(BF16)
    low = (x - high.astype(F32)).astype(BF16)
    return jnp.concatenate([high, low], axis=axis)


def down(row):
    parts = []
    for at in range(0, row.shape[1], LANES):
        piece = jnp.broadcast_to(row[:, at : at + LANES], (LANES, LANES))
        parts.append(piece.T)
    return jnp.concatenate(parts, axis=0)


def cols(head, count=1):
    return slice(head * LANES, (head + count) * LANES)


def pack(send_ref, head, update, extra):
    for quarter in range(4):
        first = (head * 4 + quarter) * PIECE
        send_ref[first : first + QUARTER, :] = update[quarter * QUARTER : (quarter + 1) * QUARTER]
        send_ref[first + QUARTER : first + PIECE, :] = extra


def row_copies(src, dst, sems):
    return [
        pltpu.make_async_copy(src.at[cols(part)], dst.at[cols(part)], sems.at[part])
        for part in range(src.shape[0] // LANES)
    ]


def intra(cumul_ref, k_ref, v_ref, q_ref, table_ref, probs_ref, intra_ref, grow_ref, tail_ref, pull_ref):
    heads, tokens = cumul_ref.shape
    place_t = lax.broadcasted_iota(jnp.int32, (LANES, LANES), 0)
    place_s = lax.broadcasted_iota(jnp.int32, (LANES, LANES), 1)
    lower = place_t >= place_s
    empty = jnp.zeros((LANES, LANES), F32)
    for head in range(heads):
        row = cumul_ref[head : head + 1, :]
        last = row[:, tokens - 1 :]
        column = down(row)
        mine = cols(head)
        grow_ref[:, mine] = jnp.exp(column)
        tail_ref[:, mine] = jnp.exp(last - column)
        pull_ref[head] = halves(q_ref[:, mine].T.astype(F32) * jnp.exp(row), 0)
        for at in range(0, tokens, TALL):
            end = at + TALL
            bands = []
            for t in range(at // LANES, end // LANES):
                tiles = []
                for s in range(end // LANES):
                    spread = column[cols(t)] - row[:, cols(s)]
                    if s < t:
                        tiles.append(jnp.exp(spread))
                    else:
                        tiles.append(jnp.where(lower, jnp.exp(spread), F32(0.0)) if s == t else empty)
                bands.append(jnp.concatenate(tiles, axis=1))
            weights = jnp.concatenate(bands, axis=0)
            table_ref[head, at:end, :end] = weights
            scores = contract(q_ref[at:end, mine], k_ref[:end, mine], 1, 1)
            probs = (weights * scores).astype(BF16)
            probs_ref[head, :end, at:end] = probs.T
            intra_ref[at:end, mine] = contract(probs, v_ref[:end, mine], 1, 0)


def front_kernel(
    core_ref, a_hbm, k_hbm, v_hbm, q_hbm, og_hbm,
    cumul_ref, send_ref, k_ref, v_ref, table_ref, probs_ref, intra_ref, grow_ref, tail_ref, pull_ref, q_ref, og_ref,
    a_ref, update_ref, a_sem, sems,
):
    heads, tokens = a_ref.shape
    a_copy = pltpu.make_async_copy(a_hbm, a_ref, a_sem)
    a_copy.start()
    k_copies = row_copies(k_hbm, k_ref, sems.at[0])
    v_copies = row_copies(v_hbm, v_ref, sems.at[1])
    late = row_copies(q_hbm, q_ref, sems.at[2]) + row_copies(og_hbm, og_ref, sems.at[3])
    for part in range(tokens // LANES):
        k_copies[part].start()
        v_copies[part].start()

    @pl.when(core_ref[0] == 0)
    def _():
        for copy in late:
            copy.start()

    place_s = lax.broadcasted_iota(jnp.int32, (LANES, LANES), 0)
    place_t = lax.broadcasted_iota(jnp.int32, (LANES, LANES), 1)
    upper = (place_s <= place_t).astype(F32)
    before = jnp.zeros((heads, 1), F32)
    a_copy.wait()
    for at in range(0, tokens, LANES):
        piece = contract(a_ref[:, at : at + LANES], upper, 1, 0, HIGH) + before
        before = piece[:, LANES - 1 :]
        cumul_ref[:, at : at + LANES] = piece
    for at in range(0, tokens, TALL):
        end = at + TALL
        for copies in (k_copies, v_copies):
            for copy in copies[at // LANES : end // LANES]:
                copy.wait()
        for head in range(heads):
            mine = cols(head)
            row = cumul_ref[head : head + 1, :]
            last = row[:, tokens - 1 :]
            k_tail = k_ref[at:end, mine].T.astype(F32) * jnp.exp(last - row[:, at:end])
            both = contract(halves(k_tail, 0), v_ref[at:end, mine], 1, 0)
            update = both[:LANES] + both[LANES:]
            if at:
                update = update + update_ref[head]
            if end < tokens:
                update_ref[head] = update
            else:
                pack(send_ref, head, update, jnp.broadcast_to(last, (1, LANES)))

    @pl.when(core_ref[0] == 0)
    def _():
        for copy in late[:4]:
            copy.wait()
        intra(cumul_ref, k_ref, v_ref, q_ref, table_ref, probs_ref, intra_ref, grow_ref, tail_ref, pull_ref)
        for copy in late[4:]:
            copy.wait()


def attn_kernel(
    core_ref, q_hbm, og_hbm, cumul_ref, k_ref, v_ref, state_ref, gain_ref,
    table_ref, probs_ref, intra_ref, grow_ref, tail_ref, pull_ref, q_ref, og_ref, attn_ref, sums_ref,
    sq_ref, gd_ref, sems,
):
    @pl.when(core_ref[0] == 1)
    def _():
        late = row_copies(q_hbm, q_ref, sems.at[0]) + row_copies(og_hbm, og_ref, sems.at[1])
        for copy in late:
            copy.start()
        for copy in late[:4]:
            copy.wait()
        intra(cumul_ref, k_ref, v_ref, q_ref, table_ref, probs_ref, intra_ref, grow_ref, tail_ref, pull_ref)
        for copy in late[4:]:
            copy.wait()

    for at in range(0, state_ref.shape[0], GROUP):
        squares = jnp.zeros(sq_ref.shape, F32) if at == 0 else sq_ref[...]
        gdot = jnp.zeros(gd_ref.shape, F32) if at == 0 else gd_ref[...]
        for head in range(at, at + GROUP):
            mine = cols(head)
            q_one = q_ref[:, mine]
            carried = contract(jnp.concatenate([q_one, q_one], axis=1), halves(state_ref[head], 0), 1, 0)
            attn = intra_ref[:, mine] + grow_ref[:, mine] * carried
            attn_ref[:, mine] = attn
            squares = squares + attn * attn
            gdot = gdot + gain_ref[:, mine] * og_ref[:, mine].astype(F32) * attn
        sq_ref[...] = squares
        gd_ref[...] = gdot
    ones = jnp.ones((8, LANES), F32)
    sq_row = contract(ones, sq_ref[...], 1, 1, HIGH)
    gd_row = contract(ones, gd_ref[...], 1, 1, HIGH)
    pieces = [sq_row[:1, at : at + LANES] for at in range(0, BLOCK, LANES)]
    pieces += [gd_row[:1, at : at + LANES] for at in range(0, BLOCK, LANES)]
    whole = jnp.concatenate(pieces, axis=0)
    sums_ref[...] = jnp.broadcast_to(whole[None], sums_ref.shape)


def intra_back(
    q_ref, k_ref, v_ref, grad_ref, table_ref, probs_ref, state_ref, grow_ref, attn_ref, gain_ref, inv_ref,
    dq_hbm, normed_hbm, dk_ref, dv_ref, dq_ref, normed_ref, errs_ref, sems,
):
    heads, tokens = table_ref.shape[:2]
    copies = row_copies(normed_ref, normed_hbm, sems.at[0])
    for part in range(tokens // LANES):
        rows = cols(part)
        inv_rms = jnp.concatenate([inv_ref[rows, :]] * heads, axis=1)
        normed_ref[rows, :] = (attn_ref[rows, :] * inv_rms * gain_ref[...]).astype(BF16)
        copies[part].start()
    dq_copies = row_copies(dq_ref, dq_hbm, sems.at[1])
    for at in range(0, tokens, TALL):
        end = at + TALL
        for head in range(heads):
            mine = cols(head)
            grad = grad_ref[at:end, mine]
            scores = contract(grad, v_ref[:end, mine], 1, 1)
            errs = (table_ref[head, at:end, :end] * scores).astype(BF16)
            errs_ref[head, at:end, :end] = errs
            carried = contract(jnp.concatenate([grad, grad], axis=1), halves(state_ref[head], 1), 1, 1)
            dq = contract(errs, k_ref[:end, mine], 1, 0) + grow_ref[at:end, mine] * carried
            dq_ref[at:end, mine] = dq.astype(BF16)
        for part in range(at // LANES, end // LANES):
            dq_copies[part].start()
    for head in range(heads):
        mine = cols(head)
        for at in range(0, tokens, TALL):
            end = at + TALL
            dk_ref[at:end, mine] = contract(errs_ref[head, at:, at:end], q_ref[at:, mine], 0, 0)
            dv_ref[at:end, mine] = contract(probs_ref[head, at:end, at:], grad_ref[at:, mine], 1, 0)
    return copies + dq_copies


def grad_kernel(
    features, core_ref, q_ref, k_ref, v_ref, table_ref, probs_ref, state_ref, grow_ref, attn_ref, gain_ref,
    pull_ref, og_ref, sums_ref,
    grad_ref, send_ref, inv_ref, dq_hbm, normed_hbm, dk_ref, dv_ref, back_ref, dq_ref, normed_ref, errs_ref, sems,
):
    whole = jnp.sum(sums_ref[...], axis=0)
    inv_rms = lax.rsqrt(whole[:4] / features + EPSILON)
    back = inv_rms * inv_rms * inv_rms * whole[4:] / features
    for at in range(4):
        inv_ref[cols(at), :] = jnp.broadcast_to(inv_rms[at : at + 1], (LANES, LANES)).T
        back_ref[cols(at), :] = jnp.broadcast_to(back[at : at + 1], (LANES, LANES)).T
    for head in range(pull_ref.shape[0]):
        mine = cols(head)
        og = og_ref[:, mine].astype(F32)
        grad = inv_ref[...] * gain_ref[:, mine] * og - attn_ref[:, mine] * back_ref[...]
        grad = grad.astype(BF16)
        grad_ref[:, mine] = grad
        both = contract(pull_ref[head], grad, 1, 0)
        update = both[:LANES] + both[LANES:]
        gain_part = jnp.sum(og * (attn_ref[:, mine] * inv_ref[...]), axis=0, keepdims=True)
        pack(send_ref, head, update, gain_part)

    @pl.when(core_ref[0] == 0)
    def _():
        copies = intra_back(
            q_ref, k_ref, v_ref, grad_ref, table_ref, probs_ref, state_ref, grow_ref, attn_ref, gain_ref, inv_ref,
            dq_hbm, normed_hbm, dk_ref, dv_ref, dq_ref, normed_ref, errs_ref, sems,
        )
        for copy in copies:
            copy.wait()


def finish_kernel(
    core_ref, q_ref, k_ref, v_ref, table_ref, probs_ref, state_ref, grow_ref, attn_ref, gain_ref, grad_ref, inv_ref,
    tail_ref, flow_ref,
    dq_hbm, normed_hbm, dk32_ref, dv32_ref, dk_hbm, dv_hbm, gain_grad_ref,
    dq_ref, normed_ref, dk_ref, dv_ref, errs_ref, wide_ref, high_ref, sems,
):
    @pl.when(core_ref[0] == 1)
    def _():
        intra_back(
            q_ref, k_ref, v_ref, grad_ref, table_ref, probs_ref, state_ref, grow_ref, attn_ref, gain_ref, inv_ref,
            dq_hbm, normed_hbm, dk32_ref, dv32_ref, dq_ref, normed_ref, errs_ref, sems,
        )

    heads, tokens = table_ref.shape[:2]
    for head in range(heads):
        firsts = [(head * 4 + quarter) * PIECE for quarter in range(4)]
        flow = jnp.concatenate([flow_ref[first : first + QUARTER, :] for first in firsts], axis=0)
        wide_ref[head] = halves(flow, 1)
        high_ref[head] = halves(flow, 0)
        gain_grad_ref[head : head + 1, :] = flow_ref[firsts[0] + QUARTER : firsts[0] + PIECE, :]
    dk_copies = row_copies(dk_ref, dk_hbm, sems.at[2])
    dv_copies = row_copies(dv_ref, dv_hbm, sems.at[3])
    for part in range(tokens // LANES):
        rows = cols(part)
        for head in range(heads):
            mine = cols(head)
            k_one, v_one = k_ref[rows, mine], v_ref[rows, mine]
            dk = contract(jnp.concatenate([v_one, v_one], axis=1), wide_ref[head], 1, 1)
            dv = contract(jnp.concatenate([k_one, k_one], axis=1), high_ref[head], 1, 0)
            tail = tail_ref[rows, mine]
            dk_ref[rows, mine] = (dk32_ref[rows, mine] + tail * dk).astype(BF16)
            dv_ref[rows, mine] = (dv32_ref[rows, mine] + tail * dv).astype(BF16)
        dk_copies[part].start()
        dv_copies[part].start()

    @pl.when(core_ref[0] == 1)
    def _():
        for copy in row_copies(normed_ref, normed_hbm, sems.at[0]) + row_copies(dq_ref, dq_hbm, sems.at[1]):
            copy.wait()

    for copy in dk_copies + dv_copies:
        copy.wait()


def scan_kernel(got_ref, out_ref, through_ref):
    count = out_ref.shape[0]
    state = jnp.zeros((QUARTER, LANES), F32)
    for at in range(count):
        out_ref[at] = state
        first = at * PIECE
        through = jnp.exp(got_ref[first + QUARTER : first + PIECE, :])
        through_ref[at : at + 1, :] = through
        state = through * state + got_ref[first : first + QUARTER, :]


def scan_back_kernel(got_ref, through_ref, out_ref):
    count = through_ref.shape[0]
    state = jnp.zeros((QUARTER, LANES), F32)
    gain = jnp.zeros((1, LANES), F32)
    for at in reversed(range(count)):
        first = at * PIECE
        out_ref[first : first + QUARTER, :] = state
        state = through_ref[at : at + 1, :] * state + got_ref[first : first + QUARTER, :]
        gain = gain + got_ref[first + QUARTER : first + PIECE, :]
    for at in range(count):
        out_ref[at * PIECE + QUARTER : (at + 1) * PIECE, :] = gain


def call(kernel, name, ins, outs, scratch=(), into=None):
    place = lambda space: pl.BlockSpec(memory_space=space)
    pin = lambda array, space: pltpu.with_memory_space_constraint(array, space) if space == pltpu.HBM else array
    spaces = [space for _, space in ins]
    arrays = [pin(array, space) for array, space in ins]
    aliases = {}
    body = kernel
    if into is not None:
        known, count = len(ins), len(into)
        aliases = {known + at: at for at in range(count)}
        spaces += [space for _, _, space in outs[:count]]
        arrays += [pin(array, space) for array, (_, _, space) in zip(into, outs)]
        body = lambda *refs: kernel(*refs[:known], *refs[known + count :])
    return pl.pallas_call(
        body,
        in_specs=[place(space) for space in spaces],
        out_specs=[place(space) for _, _, space in outs],
        out_shape=[jax.ShapeDtypeStruct(shape, dtype) for shape, dtype, _ in outs],
        scratch_shapes=list(scratch),
        input_output_aliases=aliases,
        compiler_params=pltpu.CompilerParams(vmem_limit_bytes=VMEM_LIMIT),
        name=name,
    )(*arrays)


def exchange(x):
    return lax.all_to_all(x.reshape(-1), "seq", 0, 0, tiled=True).reshape(x.shape)


def on_device(queries, key_vecs, value_vecs, log_decay, norm_gain, out_grad):
    tokens, wide = queries.shape
    heads = log_decay.shape[1]
    ring = lax.axis_size("seq")
    others = lax.axis_size("dp")
    features = wide * others
    parts = tokens // LANES
    gain_row = norm_gain.reshape(1, wide)
    vm, hbm = pltpu.VMEM, pltpu.HBM
    core = ((lax.axis_index("dp") & 1).astype(jnp.int32).reshape(1), pltpu.SMEM)
    flat = (tokens, wide)
    square = (heads, tokens, tokens)
    packed = (ring * PIECE, LANES)

    inside_outs = [
        (square, F32, vm),
        (square, BF16, vm),
        (flat, F32, vm),
        (flat, F32, vm),
        (flat, F32, vm),
        ((heads, 2 * LANES, tokens), BF16, vm),
        (flat, BF16, vm),
        (flat, BF16, vm),
    ]
    cumul, send, k, v, *inside = call(
        front_kernel,
        "front",
        [core, (log_decay.T, hbm), (key_vecs, hbm), (value_vecs, hbm), (queries, hbm), (out_grad, hbm)],
        [((heads, tokens), F32, vm), (packed, F32, vm), (flat, BF16, vm), (flat, BF16, vm)] + inside_outs,
        [
            pltpu.VMEM((heads, tokens), F32),
            pltpu.VMEM((heads, LANES, LANES), F32),
            pltpu.SemaphoreType.DMA,
            pltpu.SemaphoreType.DMA((4, parts)),
        ],
    )
    before, through = call(
        scan_kernel,
        "scan",
        [(exchange(send), vm)],
        [((ring, QUARTER, LANES), F32, vm), ((ring, LANES), F32, vm)],
    )
    state_in = exchange(before).reshape(heads, LANES, LANES)
    *inside, attn, sums = call(
        attn_kernel,
        "attn",
        [core, (queries, hbm), (out_grad, hbm), (cumul, vm), (k, vm), (v, vm), (state_in, vm), (gain_row, vm)],
        inside_outs + [(flat, F32, vm), ((others, 8, LANES), F32, vm)],
        [pltpu.VMEM((tokens, LANES), F32)] * 2 + [pltpu.SemaphoreType.DMA((2, parts))],
        inside,
    )
    table, probs, intra_attn, grow, tail, pull, q, og = inside
    sums = lax.all_to_all(sums, "dp", 0, 0, tiled=True)
    block_ins = [
        core, (q, vm), (k, vm), (v, vm), (table, vm), (probs, vm), (state_in, vm), (grow, vm), (attn, vm), (gain_row, vm)
    ]
    block_outs = [(flat, BF16, hbm), (flat, BF16, hbm), (flat, F32, vm), (flat, F32, vm)]
    grad, send, inv_rms, *inside = call(
        functools.partial(grad_kernel, features),
        "grad",
        block_ins + [(pull, vm), (og, vm), (sums, vm)],
        [(flat, BF16, vm), (packed, F32, vm), ((tokens, LANES), F32, vm)] + block_outs,
        [
            pltpu.VMEM((tokens, LANES), F32),
            pltpu.VMEM(flat, BF16),
            pltpu.VMEM(flat, BF16),
            pltpu.VMEM(square, BF16),
            pltpu.SemaphoreType.DMA((2, parts)),
        ],
    )
    after = call(
        scan_back_kernel, "scan_back", [(exchange(send), vm), (through, vm)], [(packed, F32, vm)]
    )[0]
    dq, normed, _, _, dk, dv, gain_grad = call(
        finish_kernel,
        "finish",
        block_ins + [(grad, vm), (inv_rms, vm), (tail, vm), (exchange(after), vm)],
        block_outs + [(flat, BF16, hbm), (flat, BF16, hbm), ((heads, LANES), F32, vm)],
        [pltpu.VMEM(flat, BF16)] * 4
        + [
            pltpu.VMEM(square, BF16),
            pltpu.VMEM((heads, LANES, 2 * LANES), BF16),
            pltpu.VMEM((heads, 2 * LANES, LANES), BF16),
            pltpu.SemaphoreType.DMA((4, parts)),
        ],
        inside,
    )
    return normed, dq, dk, dv, gain_grad.reshape(wide)


def solution(mesh):
    placed = (
        P("seq", "dp"),
        P("seq", "dp"),
        P("seq", "dp"),
        P("seq", "dp"),
        P("dp"),
        P("seq", "dp"),
    )
    return jax.shard_map(
        on_device,
        mesh=mesh,
        in_specs=placed,
        out_specs=(P("seq", "dp"), P("seq", "dp"), P("seq", "dp"), P("seq", "dp"), P("dp")),
        check_vma=False,
    )
```
